256 devices in a mesh: frames: 4 (over x), space: 64 (over z, y, core).
Axes of the slice: x: 4, y: 4, z: 8, core: 2. Of those that a mesh axis runs over, the one named last changes fastest.
Arguments:
- queries: bfloat16 [65536, 2240], P(('frames', 'space')), may hold values from -6 to 6
- key_inputs: bfloat16 [65536, 2240], P(('frames', 'space')), may hold values from -6 to 6
- value_inputs: bfloat16 [65536, 2240], P(('frames', 'space')), may hold values from -10 to 10
- out_cotangent: bfloat16 [65536, 2240], P(('frames', 'space')), may hold values from -3072 to 3072
- frame_ids: int32 [65536], P(('frames', 'space')), may hold values from 0 to 1, as said below
Outputs:
- grad_queries: bfloat16 [65536, 2240], P(('frames', 'space'))
- grad_keys: bfloat16 [65536, 2240], P(('frames', 'space'))
- grad_values: bfloat16 [65536, 2240], P(('frames', 'space'))
The draws below stay inside these ranges and needn't reach their ends.
Inputs may be any that keep to these rules, and one draw needn't show every extreme that they name: `frame_ids`: on each device's 256 tokens the numbers never fall; the first is 0 and the last 1.
All inputs are finite; a program needn't handle non-finite values.
Results may differ from the reference program's by a relative error of at most 0.002.
Values sent between devices are 32-bit elements; how exact they have to be, the bound alone decides.
No kernel may reach another device: no remote copies, remote signals or barrier semaphores. Data moves between devices by JAX's collectives and lax.ppermute only.
A program may use at most 128 MiB of HBM per device.

```python
import jax
import jax.numpy as jnp
from jax import lax

H = 20
E = 112
D = 2240
FG = 2
TOK_DEV = 256
TOKENS = 65536
N_FRAMES = 4


def draw_frame_ids(key, part):
    key = jax.random.fold_in(key, 7)
    blocks = TOKENS // TOK_DEV
    cuts = jax.random.randint(key, (blocks, FG - 1), 1, TOK_DEV)
    cuts = jnp.sort(cuts, axis=1)
    position = jnp.arange(TOK_DEV, dtype=jnp.int32)
    frame_ids = jnp.sum((position[None, :, None] >= cuts[:, None, :]).astype(jnp.int32), axis=2)
    return frame_ids.reshape(TOKENS).astype(jnp.int32)


def draw_value_inputs(key, part):
    key = jax.random.fold_in(key, 11)
    offset_key, noise_key = jax.random.split(key, 2)
    offset = jnp.clip(0.5 * jax.random.normal(offset_key, (D,), jnp.float32), -2.0, 2.0)
    noise = jnp.clip(jax.random.normal(noise_key, (TOKENS, D), jnp.float32), -6.0, 6.0)
    return (offset[None, :] + noise).astype(jnp.bfloat16)


def block_levels(stream_key, dims, shards, smallest, largest):
    factor_of = 1.0
    for axis_at, shards_of in shards:
        steps = jax.random.uniform(jax.random.fold_in(jax.random.fold_in(stream_key, 6), axis_at), (shards_of,), jnp.float32, smallest / len(shards), largest / len(shards))
        factor_of = factor_of * jnp.repeat(jnp.exp(steps), dims[axis_at] // shards_of).reshape((-1,) + (1,) * (len(dims) - 1 - axis_at))
    return factor_of


def centred(key, dims, scale, most, shards=(), kind=jnp.bfloat16):
    result = jax.random.normal(key, dims, jnp.float32) * scale
    if len(shards) > 0:
        result = block_levels(key, dims, shards, -0.22, 0.18) * result
    return jnp.clip(result, min=-most, max=most).astype(kind)


def setup_inputs(seed: int = 0) -> dict:
    seeds = jax.random.split(jax.random.key(seed), 6)
    queries = centred(seeds[0], (TOKENS, D), 1.0, 6.0, ((0, 256),))
    key_inputs = centred(seeds[1], (TOKENS, D), 1.0, 6.0, ((0, 256),))
    value_inputs = draw_value_inputs(jax.random.fold_in(seeds[5], 71), 0)
    out_cotangent = centred(seeds[3], (TOKENS, D), (2 * TOKENS ** 0.5), 3072.0, ((0, 256),))
    frame_ids = draw_frame_ids(jax.random.fold_in(seeds[5], 71), 0)
    return {"queries": queries, "key_inputs": key_inputs, "value_inputs": value_inputs, "out_cotangent": out_cotangent, "frame_ids": frame_ids}


HIGH = lax.Precision.HIGHEST

def forward(query_in, key_in, value_in, frame_ids):
    length = TOKENS // N_FRAMES
    shape = (N_FRAMES, length, H, E)
    phi_query = jax.nn.relu(query_in).reshape(shape)
    phi_key = jax.nn.relu(key_in).reshape(shape)
    values = value_in.reshape(shape)
    masks = (frame_ids.reshape(N_FRAMES, length)[..., None] == jnp.arange(FG, dtype=jnp.int32)).astype(jnp.float32)
    states = []
    sums = []
    for frame in range(FG):
        masked = phi_key * masks[..., frame][..., None, None]
        states.append(jnp.einsum('glhe,glhd->ghed', masked, values, precision=HIGH))
        sums.append(lax.optimization_barrier(jnp.sum(masked, axis=1)))
    states = jnp.stack(states, 1).reshape(N_FRAMES * FG, H, E, E)
    sums = jnp.stack(sums, 1).reshape(N_FRAMES * FG, H, E)
    cumulative = jnp.cumsum(states, axis=0).reshape(N_FRAMES, FG, H, E, E)
    cum_sums = jnp.cumsum(sums, axis=0).reshape(N_FRAMES, FG, H, E)
    numer = jnp.zeros(shape, jnp.float32)
    denom = jnp.ones((N_FRAMES, length, H), jnp.float32)
    for frame in range(FG):
        masked = phi_query * masks[..., frame][..., None, None]
        numer = numer + jnp.einsum('glhe,ghed->glhd', masked, cumulative[:, frame], precision=HIGH)
        denom = denom + jnp.einsum('glhe,ghe->glh', masked, cum_sums[:, frame], precision=HIGH)
    return (numer / denom[..., None]).reshape(TOKENS, H * E)

def reference(queries, key_inputs, value_inputs, out_cotangent, frame_ids):

    def wrapped(query_in, key_in, value_in):
        return forward(query_in, key_in, value_in, frame_ids)
    _, pullback = jax.vjp(wrapped, queries.astype(jnp.float32), key_inputs.astype(jnp.float32), value_inputs.astype(jnp.float32))
    gradients = pullback(out_cotangent.astype(jnp.float32))
    return (gradients[0].astype(jnp.bfloat16), gradients[1].astype(jnp.bfloat16), gradients[2].astype(jnp.bfloat16))
```

```python
import jax
import jax.numpy as jnp
from jax import lax
from jax.experimental import pallas as pl
from jax.experimental.pallas import tpu as pltpu
from jax.sharding import Mesh, PartitionSpec as P

H = 20
E = 112
FG = 2
LANES = 128
CORES = 2
HALF = H // CORES
F32 = jnp.float32
BF16 = jnp.bfloat16
VMEM_LIMIT = 40 * 1024 * 1024


def frame_rows(ids_ref, count):
    zeros = (ids_ref[...] == 0).astype(F32)
    first = jnp.sum(jnp.sum(zeros, axis=1, keepdims=True), axis=0, keepdims=True)
    row = lax.broadcasted_iota(jnp.int32, (count, LANES), 0).astype(F32)
    early = row < first
    mask = early.astype(F32)
    return early, mask.astype(BF16), (1.0 - mask).astype(BF16)


def by_frame(rows, first, second):
    return jnp.concatenate([rows * first, rows * second], axis=1)


def split(values):
    high = values.astype(BF16)
    return high, (values - high.astype(F32)).astype(BF16)


def head(ref, h):
    return ref[:, h * E : (h + 1) * E]


def widen(rows):
    return jnp.concatenate([rows, jnp.ones((rows.shape[0], LANES - E), rows.dtype)], axis=1)


def over_tokens(left, right):
    return lax.dot_general(left, right, (((0,), (0,)), ((), ())), preferred_element_type=F32)


def plain(left, right):
    return jnp.dot(left, right, preferred_element_type=F32)


def transposed(left, right):
    return lax.dot_general(left, right, (((1,), (1,)), ((), ())), preferred_element_type=F32)


def put(core, h, block, keep_ref, send_ref):
    rows = pl.ds((h % HALF) * E, E)

    @pl.when(core == h // HALF)
    def _():
        keep_ref[rows, :] = block

    @pl.when(core != h // HALF)
    def _():
        send_ref[rows, :] = block


def get(core, h, mine_ref, other_ref):
    rows = pl.ds((h % HALF) * E, E)
    return jnp.where(core == h // HALF, mine_ref[rows, :], other_ref[rows, :])


def key_kernel(ids_ref, key_ref, value_ref, keep_ref, send_ref):
    core = lax.axis_index("core")
    _, first, second = frame_rows(ids_ref, key_ref.shape[0])
    for h in range(H):
        phi = jnp.maximum(head(key_ref, h), 0)
        values = by_frame(widen(head(value_ref, h)), first, second)
        put(core, h, over_tokens(phi, values), keep_ref, send_ref)


def query_kernel(ids_ref, query_ref, cot_ref, mine_ref, other_ref, grad_ref, keep_ref, send_ref):
    core = lax.axis_index("core")
    count = query_ref.shape[0]
    early, first, second = frame_rows(ids_ref, count)
    for h in range(H):
        high, low = split(get(core, h, mine_ref, other_ref))
        query = head(query_ref, h)
        phi = jnp.maximum(query, 0)
        both = plain(phi, high) + plain(phi, low)
        numer = jnp.where(early, both[:, :LANES], both[:, LANES:])
        inverse = 1.0 / (numer[:, E : E + 1] + 1.0)
        cot = head(cot_ref, h)
        wide = cot.astype(F32)
        inner = -jnp.sum(wide * numer[:, :E], axis=1, keepdims=True) * inverse
        grads = jnp.concatenate(
            [wide * inverse, inner * inverse, jnp.zeros((count, LANES - E - 1), F32)], axis=1
        )
        grads_high, grads_low = split(grads)
        block = over_tokens(phi, by_frame(grads_high, first, second)) + over_tokens(
            phi, by_frame(grads_low, first, second)
        )
        put(core, h, block, keep_ref, send_ref)
        inner_high, rest = split(inner)
        inner_mid = (inner - inner_high.astype(F32)).astype(BF16)
        inner_low = (inner - inner_high.astype(F32) - inner_mid.astype(F32)).astype(BF16)
        left = jnp.concatenate(
            [cot, inner_high, inner_mid, inner_low, jnp.zeros((count, LANES - E - 3), BF16)], axis=1
        )
        left = by_frame(left, first, second)
        grad = (transposed(left, high) + transposed(left, low)) * inverse
        grad_ref[:, h * E : (h + 1) * E] = jnp.where(query.astype(F32) > 0, grad, 0.0).astype(BF16)


def value_kernel(ids_ref, key_ref, value_ref, mine_ref, other_ref, grad_key_ref, grad_value_ref):
    core = lax.axis_index("core")
    early, first, second = frame_rows(ids_ref, key_ref.shape[0])
    for h in range(H):
        high, low = split(get(core, h, mine_ref, other_ref))
        key = head(key_ref, h)
        phi = jnp.maximum(key, 0)
        both = plain(phi, high) + plain(phi, low)
        grad = jnp.where(early, both[:, :LANES], both[:, LANES:])
        grad_value_ref[:, h * E : (h + 1) * E] = grad[:, :E].astype(BF16)
        values = by_frame(widen(head(value_ref, h)), first, second)
        grad = transposed(values, high) + transposed(values, low)
        grad_key_ref[:, h * E : (h + 1) * E] = jnp.where(key.astype(F32) > 0, grad, 0.0).astype(BF16)


def call(kernel, outs, *operands):
    return pl.pallas_call(
        kernel,
        out_shape=outs,
        compiler_params=pltpu.CompilerParams(vmem_limit_bytes=VMEM_LIMIT),
    )(*operands)


def swap_cores(block):
    return lax.ppermute(block, "core", [(0, 1), (1, 0)])


def exchange(block, axis):
    return lax.all_to_all(block, axis, 0, 0, tiled=False)


def carried(keep, send, backward):
    y, z, frames = lax.axis_size("y"), lax.axis_size("z"), lax.axis_size("frames")
    rows = keep.shape[0] // y
    part = -(-rows // (8 * z)) * 8
    summed = (keep + swap_cores(send)).reshape(y, rows, FG * LANES)
    summed = jnp.sum(exchange(summed, "y"), axis=0)
    summed = jnp.pad(summed, ((0, z * part - rows), (0, 0))).reshape(z, part, FG * LANES)
    summed = jnp.sum(exchange(summed, "z"), axis=0)
    frame0, frame1 = summed[:, :LANES], summed[:, LANES:]
    total = frame0 + frame1
    me = lax.axis_index("frames")
    carry = jnp.zeros_like(total)
    for hop in range(1, frames):
        step = -hop if backward else hop
        moved = lax.ppermute(total, "frames", [(i, (i + step) % frames) for i in range(frames)])
        reaches = (me + hop < frames) if backward else (me >= hop)
        carry = carry + jnp.where(reaches, moved, 0.0)
    if backward:
        done = jnp.concatenate([carry + total, carry + frame1], axis=1)
    else:
        done = jnp.concatenate([carry + frame0, carry + total], axis=1)
    done = exchange(jnp.broadcast_to(done[None], (z,) + done.shape), "z")
    done = done.reshape(z * part, FG * LANES)[:rows]
    done = exchange(jnp.broadcast_to(done[None], (y,) + done.shape), "y")
    done = done.reshape(y * rows, FG * LANES)
    return done, swap_cores(done)


def on_device(queries, key_inputs, value_inputs, out_cotangent, frame_ids):
    ids = frame_ids.reshape(-1, LANES)
    states = jax.ShapeDtypeStruct((HALF * E, FG * LANES), F32)
    grads = jax.ShapeDtypeStruct(queries.shape, BF16)
    keep, send = call(key_kernel, (states, states), ids, key_inputs, value_inputs)
    mine, other = carried(keep, send, False)
    grad_queries, keep, send = call(
        query_kernel, (grads, states, states), ids, queries, out_cotangent, mine, other
    )
    mine, other = carried(keep, send, True)
    grad_keys, grad_values = call(
        value_kernel, (grads, grads), ids, key_inputs, value_inputs, mine, other
    )
    return grad_queries, grad_keys, grad_values


def solution(mesh):
    sizes = mesh.shape
    y = 4
    z = sizes["space"] // (y * CORES)
    fine = Mesh(
        mesh.devices.reshape(sizes["frames"], z, y, CORES), ("frames", "z", "y", "core")
    )
    space = ("frames", "z", "y", "core")
    rows = P(space, None)
    return jax.shard_map(
        on_device,
        mesh=fine,
        in_specs=(rows, rows, rows, rows, P(space)),
        out_specs=(rows, rows, rows),
        check_vma=False,
    )
```

```python
import jax
import jax.numpy as jnp
from jax import lax
from jax.experimental import pallas as pl
from jax.experimental.pallas import tpu as pltpu
from jax.sharding import PartitionSpec as P

H = 20
E = 112
LANES = 128
CORES = 2
HALF = H // CORES
ROWS = HALF * E
STATE_ROWS = 1152
WIDE = 2 * LANES
F32 = jnp.float32
BF16 = jnp.bfloat16
VMEM_LIMIT = 32 * 1024 * 1024
Y = 4


def frame_masks(ids_ref):
    early = ids_ref[...] == 0
    first = early.astype(F32)
    return early, first.astype(BF16), (1.0 - first).astype(BF16)


def by_frame(rows, first, second):
    return jnp.concatenate([rows * first, rows * second], axis=0)


def split(values):
    high = values.astype(BF16)
    return high, (values - high.astype(F32)).astype(BF16)


def with_ones(rows):
    return jnp.concatenate([rows, jnp.ones((LANES - E, rows.shape[1]), rows.dtype)], axis=0)


def with_rows(rows, *extra):
    at = lax.broadcasted_iota(jnp.int32, (LANES - E, rows.shape[1]), 0)
    tail = jnp.zeros((LANES - E, rows.shape[1]), F32)
    for place, row in enumerate(extra):
        tail = jnp.where(at == place, row, tail)
    return jnp.concatenate([rows, tail.astype(rows.dtype)], axis=0)


def over_tokens(left, right):
    return lax.dot_general(left, right, (((1,), (1,)), ((), ())), preferred_element_type=F32)


def over_columns(left, right):
    return jnp.dot(left, right, preferred_element_type=F32)


def over_rows(left, right):
    return lax.dot_general(left, right, (((0,), (0,)), ((), ())), preferred_element_type=F32)


def stacked(state, rows):
    return jnp.concatenate(split(state), axis=0), jnp.concatenate([rows, rows], axis=0)


def own_frame(both, early):
    return jnp.where(early, both[:LANES], both[LANES:])


def fill_up(state_ref):
    state_ref[ROWS:, :] = jnp.zeros((STATE_ROWS - ROWS, WIDE), F32)


def key_state(key, value, first, second):
    return over_tokens(jnp.maximum(key, 0), by_frame(with_ones(value), first, second))


def key_kernel(half_ref, ids_ref, key_ref, value_ref, state_ref):
    _, first, second = frame_masks(ids_ref)
    for h in range(HALF):
        rows = pl.ds(h * E, E)
        state_ref[rows, :] = key_state(key_ref[rows, :], value_ref[rows, :], first, second)
    fill_up(state_ref)


def query_kernel(half_ref, ids_ref, query_ref, cot_ref, state_ref, aux_ref, grad_state_ref):
    early, first, second = frame_masks(ids_ref)
    for h in range(HALF):
        rows = pl.ds(h * E, E)
        phi = jnp.maximum(query_ref[rows, :], 0)
        numer = own_frame(over_rows(*stacked(state_ref[rows, :], phi)), early)
        inverse = 1.0 / (numer[E : E + 1] + 1.0)
        wide = cot_ref[rows, :].astype(F32)
        inner = -jnp.sum(wide * numer[:E], axis=0, keepdims=True) * inverse
        aux_ref[h] = jnp.concatenate([inverse, inner], axis=0)
    for h in range(HALF):
        rows = pl.ds(h * E, E)
        inverse, inner = aux_ref[h, 0:1, :], aux_ref[h, 1:2, :]
        phi = by_frame(jnp.maximum(query_ref[rows, :], 0), first, second)
        wide = cot_ref[rows, :].astype(F32)
        high, low = split(with_rows(wide * inverse, inner * inverse))
        block = over_tokens(phi, high) + over_tokens(phi, low)
        grad_state_ref[rows, :] = jnp.concatenate([block[:E], block[E:]], axis=1)
    fill_up(grad_state_ref)


def query_grad_kernel(half_ref, ids_ref, query_ref, cot_ref, state_ref, aux_ref, *refs):
    grad_ref = refs[-1]
    _, first, second = frame_masks(ids_ref)
    for h in range(HALF):
        rows = pl.ds(h * E, E)
        high, low = split(state_ref[rows, :])
        inverse, inner = aux_ref[h, 0:1, :], aux_ref[h, 1:2, :]
        inner_high = inner.astype(BF16).astype(F32)
        inner_mid = (inner - inner_high).astype(BF16).astype(F32)
        inner_low = inner - inner_high - inner_mid
        cots = with_rows(cot_ref[rows, :], inner_high, inner_mid, inner_low)
        cots = by_frame(cots, first, second)
        grad = (over_columns(high, cots) + over_columns(low, cots)) * inverse
        grad_ref[rows, :] = jnp.where(query_ref[rows, :].astype(F32) > 0, grad, 0.0).astype(BF16)


def value_kernel(half_ref, ids_ref, key_ref, value_ref, state_ref, *refs):
    grad_key_ref, grad_value_ref = refs[-2:]
    early, first, second = frame_masks(ids_ref)
    for h in range(HALF):
        rows = pl.ds(h * E, E)
        state = state_ref[rows, :]
        high, low = split(state)
        key = key_ref[rows, :]
        grad = own_frame(over_rows(*stacked(state, jnp.maximum(key, 0))), early)
        grad_value_ref[rows, :] = grad[:E].astype(BF16)
        values = by_frame(with_ones(value_ref[rows, :]), first, second)
        grad = over_columns(high, values) + over_columns(low, values)
        grad_key_ref[rows, :] = jnp.where(key.astype(F32) > 0, grad, 0.0).astype(BF16)


def gather_kernel(parts_ref, sum_ref):
    rows, pieces, piece = parts_ref.shape[1], sum_ref.shape[0], sum_ref.shape[1]
    for at in range(pieces):
        filled = min(piece, rows - at * piece)
        if filled > 0:
            here = pl.ds(at * piece, filled)
            total = parts_ref[0, here, :]
            for part in range(1, parts_ref.shape[0]):
                total = total + parts_ref[part, here, :]
            sum_ref[at, :filled, :] = total
        if filled < piece:
            start = max(filled, 0)
            sum_ref[at, start:, :] = jnp.zeros((piece - start, WIDE), F32)


def params():
    return pltpu.CompilerParams(vmem_limit_bytes=VMEM_LIMIT)


def on_half(kernel, half, ids, halves, small, whole, outs):
    tokens = ids.shape[1]
    block = pl.BlockSpec((ROWS, tokens), lambda i, at: (at[0], 0))
    full = lambda shape: pl.BlockSpec(shape, lambda i, at: (0,) * len(shape))
    operands = [ids, *halves, *small, *whole]
    specs = [full(ids.shape)] + [block] * len(halves) + [full(a.shape) for a in small]
    specs += [pl.BlockSpec(memory_space=pl.ANY)] * len(whole)
    aliases = {1 + len(operands) - len(whole) + at: at for at in range(len(whole))}
    shapes = {
        "grad": ((H * E, tokens), BF16),
        "state": ((STATE_ROWS, WIDE), F32),
        "aux": ((HALF, 2, tokens), F32),
    }
    out_shape = [jax.ShapeDtypeStruct(*shapes[out]) for out in outs]
    out_specs = [block if out == "grad" else full(shapes[out][0]) for out in outs]
    return pl.pallas_call(
        kernel,
        out_shape=out_shape,
        grid_spec=pltpu.PrefetchScalarGridSpec(
            num_scalar_prefetch=1, grid=(1,), in_specs=specs, out_specs=out_specs
        ),
        input_output_aliases=aliases,
        compiler_params=params(),
        cost_estimate=pl.CostEstimate(
            flops=2 * 6 * ROWS * WIDE * tokens, bytes_accessed=4 * ROWS * tokens * 2, transcendentals=0
        ),
    )(half, *operands)


def swap_cores(block):
    return lax.ppermute(block, "space", [(i, i ^ 1) for i in range(lax.axis_size("space"))])


def groups(chips_z):
    device = lambda z, y, core: (z * Y + y) * CORES + core
    pairs = range(chips_z // 2)
    near = [
        [device(2 * pair + i, y, core) for i in range(2) for y in range(Y)]
        for core in range(CORES) for pair in pairs
    ]
    far = [
        [device(2 * pair + i, y, core) for pair in pairs]
        for core in range(CORES) for i in range(2) for y in range(Y)
    ]
    return near, far


def exchange(block, members):
    return lax.all_to_all(block, "space", 0, 0, axis_index_groups=members, tiled=False)


def carried(summed, backward, beside=None):
    frames = lax.axis_size("frames")
    near, far = groups(lax.axis_size("space") // (Y * CORES))
    chips, places = len(near[0]), len(far[0])
    rows = summed.shape[0] // chips
    part = -(-rows // (8 * places)) * 8
    summed = exchange(summed.reshape(chips, rows, WIDE), near)
    summed = pl.pallas_call(
        gather_kernel,
        out_shape=jax.ShapeDtypeStruct((places, part, WIDE), F32),
        compiler_params=params(),
    )(summed)
    summed = jnp.sum(exchange(summed, far), axis=0)
    frame0, frame1 = summed[:, :LANES], summed[:, LANES:]
    total = frame0 + frame1
    me = lax.axis_index("frames")
    carry = jnp.zeros_like(total)
    arrived = []
    for hop in range(1, frames):
        step = -hop if backward else hop
        arrived.append(
            lax.ppermute(total, "frames", [(i, (i + step) % frames) for i in range(frames)])
        )
    extra = None
    if beside is not None:
        extra = beside(total)
        arrived, extra = lax.optimization_barrier((arrived, extra))
    for hop, moved in enumerate(arrived, 1):
        reaches = (me + hop < frames) if backward else (me >= hop)
        carry = carry + jnp.where(reaches, moved, 0.0)
    if backward:
        done = jnp.concatenate([carry + total, carry + frame1], axis=1)
    else:
        done = jnp.concatenate([carry + frame0, carry + total], axis=1)
    done = exchange(jnp.broadcast_to(done[None], (places,) + done.shape), far)
    done = done.reshape(places * part, WIDE)[:rows]
    done = exchange(jnp.broadcast_to(done[None], (chips,) + done.shape), near)
    return done.reshape(chips * rows, WIDE), extra


def on_device(queries, key_inputs, value_inputs, out_cotangent, frame_ids):
    ids = frame_ids.reshape(1, -1)
    query, key, value, cot = (a.T for a in (queries, key_inputs, value_inputs, out_cotangent))
    core = (lax.axis_index("space") % CORES).astype(jnp.int32).reshape(1)
    there = 1 - core
    (send,) = on_half(key_kernel, there, ids, (key, value), (), (), ("state",))
    received = swap_cores(send)
    (keep,) = on_half(key_kernel, core, ids, (key, value), (), (), ("state",))
    mine, _ = carried(keep + received, False)
    other = swap_cores(mine)
    aux_mine, keep = on_half(query_kernel, core, ids, (query, cot), (mine,), (), ("aux", "state"))
    aux, send = on_half(query_kernel, there, ids, (query, cot), (other,), (), ("aux", "state"))
    received = swap_cores(send)
    late, _ = lax.optimization_barrier((other, send))
    grads = on_half(query_grad_kernel, there, ids, (query, cot), (late, aux), (), ("grad",))
    received, grads = lax.optimization_barrier((received, grads))

    def beside(total):
        late, _ = lax.optimization_barrier((aux_mine, total))
        return on_half(query_grad_kernel, core, ids, (query, cot), (mine, late), grads, ("grad",))

    mine, (grad_query,) = carried(keep + received, True, beside)
    other = swap_cores(mine)
    grads = on_half(value_kernel, core, ids, (key, value), (mine,), (), ("grad", "grad"))
    grad_key, grad_value = on_half(
        value_kernel, there, ids, (key, value), (other,), grads, ("grad", "grad")
    )
    return grad_query.T, grad_key.T, grad_value.T


def solution(mesh):
    rows = P(("frames", "space"), None)
    return jax.shard_map(
        on_device,
        mesh=mesh,
        in_specs=(rows, rows, rows, rows, P(("frames", "space"))),
        out_specs=(rows, rows, rows),
        check_vma=False,
    )
```

```python
import jax
import jax.numpy as jnp
from jax import lax
from jax.experimental import pallas as pl
from jax.experimental.pallas import tpu as pltpu
from jax.sharding import PartitionSpec as P

H = 20
E = 112
LANES = 128
CORES = 2
HALF = H // CORES
ROWS = HALF * E
TILES = -(-ROWS // 128)
SUMS = ROWS % 128
STATE_ROWS = 1024
WIDE = 2 * LANES
F32 = jnp.float32
BF16 = jnp.bfloat16
VMEM_LIMIT = 32 * 1024 * 1024
Y = 4


def frame_masks(ids_ref):
    early = ids_ref[...] == 0
    first = early.astype(F32)
    return early, first.astype(BF16), (1.0 - first).astype(BF16)


def by_frame(rows, first, second):
    return jnp.concatenate([rows * first, rows * second], axis=0)


def split(values):
    high = values.astype(BF16)
    return high, (values - high.astype(F32)).astype(BF16)


def with_ones(rows):
    return jnp.concatenate([rows, jnp.ones((LANES - E, rows.shape[1]), rows.dtype)], axis=0)


def with_rows(rows, *extra):
    at = lax.broadcasted_iota(jnp.int32, (LANES - E, rows.shape[1]), 0)
    tail = jnp.zeros((LANES - E, rows.shape[1]), F32)
    for place, row in enumerate(extra):
        tail = jnp.where(at == place, row, tail)
    return jnp.concatenate([rows, tail.astype(rows.dtype)], axis=0)


def over_tokens(left, right):
    return lax.dot_general(left, right, (((1,), (1,)), ((), ())), preferred_element_type=F32)


def over_columns(left, right):
    return jnp.dot(left, right, preferred_element_type=F32)


def over_rows(left, right):
    return lax.dot_general(left, right, (((0,), (0,)), ((), ())), preferred_element_type=F32)


def stacked(state, rows):
    return jnp.concatenate(split(state), axis=0), jnp.concatenate([rows, rows], axis=0)


def own_frame(both, early):
    return jnp.where(early, both[:LANES], both[LANES:])


def roll(block, shift):
    return pltpu.roll(block, shift % LANES, axis=1) if shift % LANES else block


def lane_of():
    return lax.broadcasted_iota(jnp.int32, (E, LANES), 1)


def unpack(state_ref, h):
    at, start = divmod(h * E, LANES)
    lane = lane_of()
    parts = []
    for frame in range(2):
        tile = lambda j: state_ref[j * E : (j + 1) * E, frame * LANES : (frame + 1) * LANES]
        block = tile(at)
        if start + E > LANES:
            block = jnp.where(lane >= start, block, tile(at + 1))
        sums = roll(tile(TILES - 1), E - SUMS - 3 * h)
        parts.append(jnp.where(lane < E, roll(block, -start), sums))
    return jnp.concatenate(parts, axis=1)


def packer(state_ref):
    lane = lane_of()
    held = {}

    def put(j, frame, block, start):
        if (j, frame) in held:
            block = jnp.where(lane >= start, block, held[j, frame])
        held[j, frame] = block

    def write(j, frame):
        state_ref[j * E : (j + 1) * E, frame * LANES : (frame + 1) * LANES] = held[j, frame]

    def add(h, block):
        at, start = divmod(h * E, LANES)
        for frame in range(2):
            part = block[:, frame * LANES : (frame + 1) * LANES]
            moved = roll(part, start)
            put(at, frame, moved, start)
            if start + E >= LANES:
                write(at, frame)
            if start + E > LANES:
                put(at + 1, frame, moved, 0)
            put(TILES, frame, roll(part, SUMS + 3 * h - E), SUMS + 3 * h)
            if h == HALF - 1:
                put(TILES - 1, frame, held[TILES, frame], SUMS)
                write(TILES - 1, frame)

    state_ref[TILES * E :, :] = jnp.zeros((STATE_ROWS - TILES * E, WIDE), F32)
    return add


def key_state(key, value, first, second):
    return over_tokens(jnp.maximum(key, 0), by_frame(with_ones(value), first, second))


def key_kernel(half_ref, ids_ref, key_ref, value_ref, state_ref):
    _, first, second = frame_masks(ids_ref)
    add = packer(state_ref)
    for h in range(HALF):
        rows = pl.ds(h * E, E)
        add(h, key_state(key_ref[rows, :], value_ref[rows, :], first, second))


def query_kernel(half_ref, ids_ref, query_ref, cot_ref, state_ref, aux_ref, grad_state_ref):
    early, first, second = frame_masks(ids_ref)
    for h in range(HALF):
        rows = pl.ds(h * E, E)
        phi = jnp.maximum(query_ref[rows, :], 0)
        numer = own_frame(over_rows(*stacked(unpack(state_ref, h), phi)), early)
        inverse = 1.0 / (numer[E : E + 1] + 1.0)
        wide = cot_ref[rows, :].astype(F32)
        inner = -jnp.sum(wide * numer[:E], axis=0, keepdims=True) * inverse
        aux_ref[h] = jnp.concatenate([inverse, inner], axis=0)
    add = packer(grad_state_ref)
    for h in range(HALF):
        rows = pl.ds(h * E, E)
        inverse, inner = aux_ref[h, 0:1, :], aux_ref[h, 1:2, :]
        phi = by_frame(jnp.maximum(query_ref[rows, :], 0), first, second)
        wide = cot_ref[rows, :].astype(F32)
        high, low = split(with_rows(wide * inverse, inner * inverse))
        block = over_tokens(phi, high) + over_tokens(phi, low)
        add(h, jnp.concatenate([block[:E], block[E:]], axis=1))


def query_grad_kernel(half_ref, ids_ref, query_ref, cot_ref, state_ref, aux_ref, *refs):
    grad_ref = refs[-1]
    _, first, second = frame_masks(ids_ref)
    for h in range(HALF):
        rows = pl.ds(h * E, E)
        high, low = split(unpack(state_ref, h))
        inverse, inner = aux_ref[h, 0:1, :], aux_ref[h, 1:2, :]
        inner_high = inner.astype(BF16).astype(F32)
        inner_mid = (inner - inner_high).astype(BF16).astype(F32)
        inner_low = inner - inner_high - inner_mid
        cots = with_rows(cot_ref[rows, :], inner_high, inner_mid, inner_low)
        cots = by_frame(cots, first, second)
        grad = (over_columns(high, cots) + over_columns(low, cots)) * inverse
        grad_ref[rows, :] = jnp.where(query_ref[rows, :].astype(F32) > 0, grad, 0.0).astype(BF16)


def value_kernel(half_ref, ids_ref, key_ref, value_ref, state_ref, *refs):
    grad_key_ref, grad_value_ref = refs[-2:]
    early, first, second = frame_masks(ids_ref)
    for h in range(HALF):
        rows = pl.ds(h * E, E)
        state = unpack(state_ref, h)
        high, low = split(state)
        key = key_ref[rows, :]
        grad = own_frame(over_rows(*stacked(state, jnp.maximum(key, 0))), early)
        grad_value_ref[rows, :] = grad[:E].astype(BF16)
        values = with_rows(value_ref[rows, :], jnp.ones((1, key.shape[1]), F32))
        values = by_frame(values, first, second)
        grad = over_columns(high, values) + over_columns(low, values)
        grad_key_ref[rows, :] = jnp.where(key.astype(F32) > 0, grad, 0.0).astype(BF16)


def gather_kernel(parts_ref, sum_ref):
    rows, pieces, piece = parts_ref.shape[1], sum_ref.shape[0], sum_ref.shape[1]
    for at in range(pieces):
        filled = min(piece, rows - at * piece)
        if filled > 0:
            here = pl.ds(at * piece, filled)
            total = parts_ref[0, here, :]
            for part in range(1, parts_ref.shape[0]):
                total = total + parts_ref[part, here, :]
            sum_ref[at, :filled, :] = total
        if filled < piece:
            start = max(filled, 0)
            sum_ref[at, start:, :] = jnp.zeros((piece - start, WIDE), F32)


def params():
    return pltpu.CompilerParams(vmem_limit_bytes=VMEM_LIMIT)


def on_half(kernel, half, ids, halves, small, whole, outs):
    tokens = ids.shape[1]
    block = pl.BlockSpec((ROWS, tokens), lambda i, at: (at[0], 0))
    full = lambda shape: pl.BlockSpec(shape, lambda i, at: (0,) * len(shape))
    operands = [ids, *halves, *small, *whole]
    specs = [full(ids.shape)] + [block] * len(halves) + [full(a.shape) for a in small]
    specs += [pl.BlockSpec(memory_space=pl.ANY)] * len(whole)
    aliases = {1 + len(operands) - len(whole) + at: at for at in range(len(whole))}
    shapes = {
        "grad": ((H * E, tokens), BF16),
        "state": ((STATE_ROWS, WIDE), F32),
        "aux": ((HALF, 2, tokens), F32),
    }
    out_shape = [jax.ShapeDtypeStruct(*shapes[out]) for out in outs]
    out_specs = [block if out == "grad" else full(shapes[out][0]) for out in outs]
    return pl.pallas_call(
        kernel,
        out_shape=out_shape,
        grid_spec=pltpu.PrefetchScalarGridSpec(
            num_scalar_prefetch=1, grid=(1,), in_specs=specs, out_specs=out_specs
        ),
        input_output_aliases=aliases,
        compiler_params=params(),
        cost_estimate=pl.CostEstimate(
            flops=2 * 6 * ROWS * WIDE * tokens, bytes_accessed=4 * ROWS * tokens * 2, transcendentals=0
        ),
    )(half, *operands)


def swap_cores(block):
    return lax.ppermute(block, "space", [(i, i ^ 1) for i in range(lax.axis_size("space"))])


def groups(chips_z):
    device = lambda z, y, core: (z * Y + y) * CORES + core
    pairs = range(chips_z // 2)
    near = [
        [device(2 * pair + i, y, core) for i in range(2) for y in range(Y)]
        for core in range(CORES) for pair in pairs
    ]
    far = [
        [device(2 * pair + i, y, core) for pair in pairs]
        for core in range(CORES) for i in range(2) for y in range(Y)
    ]
    return near, far


def exchange(block, members):
    return lax.all_to_all(block, "space", 0, 0, axis_index_groups=members, tiled=False)


def carried(summed, backward, beside=None):
    frames = lax.axis_size("frames")
    near, far = groups(lax.axis_size("space") // (Y * CORES))
    chips, places = len(near[0]), len(far[0])
    rows = summed.shape[0] // chips
    part = -(-rows // (8 * places)) * 8
    extra = None
    if beside is not None:
        extra = beside(summed)
    summed = exchange(summed.reshape(chips, rows, WIDE), near)
    if beside is not None:
        summed, extra = lax.optimization_barrier((summed, extra))
    summed = pl.pallas_call(
        gather_kernel,
        out_shape=jax.ShapeDtypeStruct((places, part, WIDE), F32),
        compiler_params=params(),
    )(summed)
    summed = jnp.sum(exchange(summed, far), axis=0)
    frame0, frame1 = summed[:, :LANES], summed[:, LANES:]
    total = frame0 + frame1
    me = lax.axis_index("frames")
    carry = jnp.zeros_like(total)
    arrived = []
    for hop in range(1, frames):
        step = -hop if backward else hop
        arrived.append(
            lax.ppermute(total, "frames", [(i, (i + step) % frames) for i in range(frames)])
        )
    for hop, moved in enumerate(arrived, 1):
        reaches = (me + hop < frames) if backward else (me >= hop)
        carry = carry + jnp.where(reaches, moved, 0.0)
    if backward:
        done = jnp.concatenate([carry + total, carry + frame1], axis=1)
    else:
        done = jnp.concatenate([carry + frame0, carry + total], axis=1)
    done = exchange(jnp.broadcast_to(done[None], (places,) + done.shape), far)
    done = done.reshape(places * part, WIDE)[:rows]
    done = exchange(jnp.broadcast_to(done[None], (chips,) + done.shape), near)
    return done.reshape(chips * rows, WIDE), extra


def on_device(queries, key_inputs, value_inputs, out_cotangent, frame_ids):
    ids = frame_ids.reshape(1, -1)
    query, key, value, cot = (a.T for a in (queries, key_inputs, value_inputs, out_cotangent))
    core = (lax.axis_index("space") % CORES).astype(jnp.int32).reshape(1)
    there = 1 - core
    (send,) = on_half(key_kernel, there, ids, (key, value), (), (), ("state",))
    received = swap_cores(send)
    (keep,) = on_half(key_kernel, core, ids, (key, value), (), (), ("state",))
    mine, _ = carried(keep + received, False)
    other = swap_cores(mine)
    aux_mine, keep = on_half(query_kernel, core, ids, (query, cot), (mine,), (), ("aux", "state"))
    aux, send = on_half(query_kernel, there, ids, (query, cot), (other,), (), ("aux", "state"))
    received = swap_cores(send)

    def beside(summed):
        own, others, _ = lax.optimization_barrier((mine, other, summed))
        grads = on_half(query_grad_kernel, core, ids, (query, cot), (own, aux_mine), (), ("grad",))
        return on_half(query_grad_kernel, there, ids, (query, cot), (others, aux), grads, ("grad",))

    last, (grad_query,) = carried(keep + received, True, beside)
    last_other = swap_cores(last)
    grads = on_half(value_kernel, core, ids, (key, value), (last,), (), ("grad", "grad"))
    grad_key, grad_value = on_half(
        value_kernel, there, ids, (key, value), (last_other,), grads, ("grad", "grad")
    )
    return grad_query.T, grad_key.T, grad_value.T


def solution(mesh):
    rows = P(("frames", "space"), None)
    return jax.shard_map(
        on_device,
        mesh=mesh,
        in_specs=(rows, rows, rows, rows, P(("frames", "space"))),
        out_specs=(rows, rows, rows),
        check_vma=False,
    )
```

```python
import jax
import jax.numpy as jnp
from jax import lax
from jax.experimental import pallas as pl
from jax.experimental.pallas import tpu as pltpu
from jax.sharding import PartitionSpec as P

H = 20
E = 112
LANES = 128
CORES = 2
HALF = H // CORES
ROWS = HALF * E
TILES = -(-ROWS // 128)
SUMS = ROWS % 128
STATE_ROWS = 1024
WIDE = 2 * LANES
F32 = jnp.float32
BF16 = jnp.bfloat16
VMEM_LIMIT = 32 * 1024 * 1024
Y = 4


def frame_masks(ids_ref):
    early = ids_ref[...] == 0
    first = early.astype(F32)
    return early, first.astype(BF16), (1.0 - first).astype(BF16)


def by_frame(rows, first, second):
    return jnp.concatenate([rows * first, rows * second], axis=0)


def split(values):
    high = values.astype(BF16)
    return high, (values - high.astype(F32)).astype(BF16)


def with_ones(rows):
    return jnp.concatenate([rows, jnp.ones((LANES - E, rows.shape[1]), rows.dtype)], axis=0)


def with_rows(rows, *extra):
    at = lax.broadcasted_iota(jnp.int32, (LANES - E, rows.shape[1]), 0)
    tail = jnp.zeros((LANES - E, rows.shape[1]), F32)
    for place, row in enumerate(extra):
        tail = jnp.where(at == place, row, tail)
    return jnp.concatenate([rows, tail.astype(rows.dtype)], axis=0)


def over_tokens(left, right):
    return lax.dot_general(left, right, (((1,), (1,)), ((), ())), preferred_element_type=F32)


def over_columns(left, right):
    return jnp.dot(left, right, preferred_element_type=F32)


def over_rows(left, right):
    return lax.dot_general(left, right, (((0,), (0,)), ((), ())), preferred_element_type=F32)


def stacked(state, rows):
    return jnp.concatenate(split(state), axis=0), jnp.concatenate([rows, rows], axis=0)


def own_frame(both, early):
    return jnp.where(early, both[:LANES], both[LANES:])


def roll(block, shift):
    return pltpu.roll(block, shift % LANES, axis=1) if shift % LANES else block


def lane_of():
    return lax.broadcasted_iota(jnp.int32, (E, LANES), 1)


def unpack(state_ref, h):
    at, start = divmod(h * E, LANES)
    lane = lane_of()
    parts = []
    for frame in range(2):
        tile = lambda j: state_ref[j * E : (j + 1) * E, frame * LANES : (frame + 1) * LANES]
        block = tile(at)
        if start + E > LANES:
            block = jnp.where(lane >= start, block, tile(at + 1))
        sums = roll(tile(TILES - 1), E - SUMS - 3 * h)
        parts.append(jnp.where(lane < E, roll(block, -start), sums))
    return jnp.concatenate(parts, axis=1)


def packer(state_ref):
    lane = lane_of()
    held = {}

    def put(j, frame, block, start):
        if (j, frame) in held:
            block = jnp.where(lane >= start, block, held[j, frame])
        held[j, frame] = block

    def write(j, frame):
        state_ref[j * E : (j + 1) * E, frame * LANES : (frame + 1) * LANES] = held[j, frame]

    def add(h, block):
        at, start = divmod(h * E, LANES)
        for frame in range(2):
            part = block[:, frame * LANES : (frame + 1) * LANES]
            moved = roll(part, start)
            put(at, frame, moved, start)
            if start + E >= LANES:
                write(at, frame)
            if start + E > LANES:
                put(at + 1, frame, moved, 0)
            put(TILES, frame, roll(part, SUMS + 3 * h - E), SUMS + 3 * h)
            if h == HALF - 1:
                put(TILES - 1, frame, held[TILES, frame], SUMS)
                write(TILES - 1, frame)

    state_ref[TILES * E :, :] = jnp.zeros((STATE_ROWS - TILES * E, WIDE), F32)
    return add


def key_state(key, value, first, second):
    return over_tokens(jnp.maximum(key, 0), by_frame(with_ones(value), first, second))


def key_kernel(half_ref, ids_ref, key_ref, value_ref, state_ref):
    _, first, second = frame_masks(ids_ref)
    add = packer(state_ref)
    for h in range(HALF):
        rows = pl.ds(h * E, E)
        add(h, key_state(key_ref[rows, :], value_ref[rows, :], first, second))


def query_kernel(half_ref, ids_ref, query_ref, cot_ref, state_ref, aux_ref, grad_state_ref):
    early, first, second = frame_masks(ids_ref)
    for h in range(HALF):
        rows = pl.ds(h * E, E)
        phi = jnp.maximum(query_ref[rows, :], 0)
        numer = own_frame(over_rows(*stacked(unpack(state_ref, h), phi)), early)
        inverse = 1.0 / (numer[E : E + 1] + 1.0)
        wide = cot_ref[rows, :].astype(F32)
        inner = -jnp.sum(wide * numer[:E], axis=0, keepdims=True) * inverse
        aux_ref[h] = jnp.concatenate([inverse, inner], axis=0)
    add = packer(grad_state_ref)
    for h in range(HALF):
        rows = pl.ds(h * E, E)
        inverse, inner = aux_ref[h, 0:1, :], aux_ref[h, 1:2, :]
        phi = by_frame(jnp.maximum(query_ref[rows, :], 0), first, second)
        wide = cot_ref[rows, :].astype(F32)
        high, low = split(with_rows(wide * inverse, inner * inverse))
        block = over_tokens(phi, high) + over_tokens(phi, low)
        add(h, jnp.concatenate([block[:E], block[E:]], axis=1))


def query_grad_kernel(half_ref, ids_ref, query_ref, cot_ref, state_ref, aux_ref, *refs):
    grad_ref = refs[-1]
    _, first, second = frame_masks(ids_ref)
    for h in range(HALF):
        rows = pl.ds(h * E, E)
        high, low = split(unpack(state_ref, h))
        inverse, inner = aux_ref[h, 0:1, :], aux_ref[h, 1:2, :]
        inner_high = inner.astype(BF16).astype(F32)
        inner_mid = (inner - inner_high).astype(BF16).astype(F32)
        inner_low = inner - inner_high - inner_mid
        cots = with_rows(cot_ref[rows, :], inner_high, inner_mid, inner_low)
        cots = by_frame(cots, first, second)
        grad = (over_columns(high, cots) + over_columns(low, cots)) * inverse
        grad_ref[rows, :] = jnp.where(query_ref[rows, :].astype(F32) > 0, grad, 0.0).astype(BF16)


def value_kernel(half_ref, ids_ref, key_ref, value_ref, state_ref, *refs):
    grad_key_ref, grad_value_ref = refs[-2:]
    early, first, second = frame_masks(ids_ref)
    for h in range(HALF):
        rows = pl.ds(h * E, E)
        state = unpack(state_ref, h)
        high, low = split(state)
        key = key_ref[rows, :]
        grad = own_frame(over_rows(*stacked(state, jnp.maximum(key, 0))), early)
        grad_value_ref[rows, :] = grad[:E].astype(BF16)
        values = with_rows(value_ref[rows, :], jnp.ones((1, key.shape[1]), F32))
        values = by_frame(values, first, second)
        grad = over_columns(high, values) + over_columns(low, values)
        grad_key_ref[rows, :] = jnp.where(key.astype(F32) > 0, grad, 0.0).astype(BF16)


def gather_kernel(parts_ref, sum_ref):
    rows, pieces, piece = parts_ref.shape[1], sum_ref.shape[0], sum_ref.shape[1]
    for at in range(pieces):
        filled = min(piece, rows - at * piece)
        if filled > 0:
            here = pl.ds(at * piece, filled)
            total = parts_ref[0, here, :]
            for part in range(1, parts_ref.shape[0]):
                total = total + parts_ref[part, here, :]
            sum_ref[at, :filled, :] = total
        if filled < piece:
            start = max(filled, 0)
            sum_ref[at, start:, :] = jnp.zeros((piece - start, WIDE), F32)


def params():
    return pltpu.CompilerParams(vmem_limit_bytes=VMEM_LIMIT)


def on_half(kernel, half, ids, halves, small, whole, outs):
    tokens = ids.shape[1]
    block = pl.BlockSpec((ROWS, tokens), lambda i, at: (at[0], 0))
    full = lambda shape: pl.BlockSpec(shape, lambda i, at: (0,) * len(shape))
    operands = [ids, *halves, *small, *whole]
    specs = [full(ids.shape)] + [block] * len(halves) + [full(a.shape) for a in small]
    specs += [pl.BlockSpec(memory_space=pl.ANY)] * len(whole)
    aliases = {1 + len(operands) - len(whole) + at: at for at in range(len(whole))}
    shapes = {
        "grad": ((H * E, tokens), BF16),
        "state": ((STATE_ROWS, WIDE), F32),
        "aux": ((HALF, 2, tokens), F32),
    }
    out_shape = [jax.ShapeDtypeStruct(*shapes[out]) for out in outs]
    out_specs = [block if out == "grad" else full(shapes[out][0]) for out in outs]
    return pl.pallas_call(
        kernel,
        out_shape=out_shape,
        grid_spec=pltpu.PrefetchScalarGridSpec(
            num_scalar_prefetch=1, grid=(1,), in_specs=specs, out_specs=out_specs
        ),
        input_output_aliases=aliases,
        compiler_params=params(),
        cost_estimate=pl.CostEstimate(
            flops=2 * 6 * ROWS * WIDE * tokens, bytes_accessed=4 * ROWS * tokens * 2, transcendentals=0
        ),
    )(half, *operands)


def swap_cores(block):
    return lax.ppermute(block, "space", [(i, i ^ 1) for i in range(lax.axis_size("space"))])


def groups(chips_z):
    device = lambda z, y, core: (z * Y + y) * CORES + core
    pairs = range(chips_z // 2)
    near = [
        [device(2 * pair + i, y, core) for i in range(2) for y in range(Y)]
        for core in range(CORES) for pair in pairs
    ]
    far = [
        [device(2 * pair + i, y, core) for pair in pairs]
        for core in range(CORES) for i in range(2) for y in range(Y)
    ]
    return near, far


def exchange(block, members):
    return lax.all_to_all(block, "space", 0, 0, axis_index_groups=members, tiled=False)


def carried(summed, backward):
    frames = lax.axis_size("frames")
    near, far = groups(lax.axis_size("space") // (Y * CORES))
    chips, places = len(near[0]), len(far[0])
    rows = summed.shape[0] // chips
    part = -(-rows // (8 * places)) * 8
    summed = exchange(summed.reshape(chips, rows, WIDE), near)
    summed = pl.pallas_call(
        gather_kernel,
        out_shape=jax.ShapeDtypeStruct((places, part, WIDE), F32),
        compiler_params=params(),
    )(summed)
    summed = jnp.sum(exchange(summed, far), axis=0)
    frame0, frame1 = summed[:, :LANES], summed[:, LANES:]
    total = frame0 + frame1
    me = lax.axis_index("frames")
    carry = jnp.zeros_like(total)
    arrived = []
    for hop in range(1, frames):
        step = -hop if backward else hop
        arrived.append(
            lax.ppermute(total, "frames", [(i, (i + step) % frames) for i in range(frames)])
        )
    for hop, moved in enumerate(arrived, 1):
        reaches = (me + hop < frames) if backward else (me >= hop)
        carry = carry + jnp.where(reaches, moved, 0.0)
    if backward:
        done = jnp.concatenate([carry + total, carry + frame1], axis=1)
    else:
        done = jnp.concatenate([carry + frame0, carry + total], axis=1)
    done = exchange(jnp.broadcast_to(done[None], (places,) + done.shape), far)
    done = done.reshape(places * part, WIDE)[:rows]
    done = exchange(jnp.broadcast_to(done[None], (chips,) + done.shape), near)
    return done.reshape(chips * rows, WIDE)


def on_device(queries, key_inputs, value_inputs, out_cotangent, frame_ids):
    ids = frame_ids.reshape(1, -1)
    query, key, value, cot = (a.T for a in (queries, key_inputs, value_inputs, out_cotangent))
    core = (lax.axis_index("space") % CORES).astype(jnp.int32).reshape(1)
    there = 1 - core
    (send,) = on_half(key_kernel, there, ids, (key, value), (), (), ("state",))
    received = swap_cores(send)
    (keep,) = on_half(key_kernel, core, ids, (key, value), (), (), ("state",))
    mine = carried(keep + received, False)
    other = swap_cores(mine)
    aux_mine, keep = on_half(query_kernel, core, ids, (query, cot), (mine,), (), ("aux", "state"))
    other, keep = lax.optimization_barrier((other, keep))
    aux, send = on_half(query_kernel, there, ids, (query, cot), (other,), (), ("aux", "state"))
    received = swap_cores(send)
    late, late_other, _ = lax.optimization_barrier((mine, other, send))
    grads = on_half(query_grad_kernel, core, ids, (query, cot), (late, aux_mine), (), ("grad",))
    (grad_query,) = on_half(
        query_grad_kernel, there, ids, (query, cot), (late_other, aux), grads, ("grad",)
    )
    received, grad_query = lax.optimization_barrier((received, grad_query))
    last = carried(keep + received, True)
    last_other = swap_cores(last)
    grads = on_half(value_kernel, core, ids, (key, value), (last,), (), ("grad", "grad"))
    grad_key, grad_value = on_half(
        value_kernel, there, ids, (key, value), (last_other,), grads, ("grad", "grad")
    )
    return grad_query.T, grad_key.T, grad_value.T


def solution(mesh):
    rows = P(("frames", "space"), None)
    return jax.shard_map(
        on_device,
        mesh=mesh,
        in_specs=(rows, rows, rows, rows, P(("frames", "space"))),
        out_specs=(rows, rows, rows),
        check_vma=False,
    )
```

```python
import jax
import jax.numpy as jnp
from jax import lax
from jax.experimental import pallas as pl
from jax.experimental.pallas import tpu as pltpu
from jax.sharding import PartitionSpec as P

H = 20
E = 112
LANES = 128
CORES = 2
HALF = H // CORES
ROWS = HALF * E
TILES = -(-ROWS // 128)
SUMS = ROWS % 128
STATE_ROWS = 1024
WIDE = 2 * LANES
F32 = jnp.float32
BF16 = jnp.bfloat16
VMEM_LIMIT = 32 * 1024 * 1024
Y = 4


def frame_masks(ids_ref):
    early = ids_ref[...] == 0
    first = early.astype(F32)
    return early, first.astype(BF16), (1.0 - first).astype(BF16)


def by_frame(rows, first, second):
    return jnp.concatenate([rows * first, rows * second], axis=0)


def split(values):
    high = values.astype(BF16)
    return high, (values - high.astype(F32)).astype(BF16)


def with_ones(rows):
    return jnp.concatenate([rows, jnp.ones((LANES - E, rows.shape[1]), rows.dtype)], axis=0)


def with_rows(rows, *extra):
    at = lax.broadcasted_iota(jnp.int32, (LANES - E, rows.shape[1]), 0)
    tail = jnp.zeros((LANES - E, rows.shape[1]), F32)
    for place, row in enumerate(extra):
        tail = jnp.where(at == place, row, tail)
    return jnp.concatenate([rows, tail.astype(rows.dtype)], axis=0)


def over_tokens(left, right):
    return lax.dot_general(left, right, (((1,), (1,)), ((), ())), preferred_element_type=F32)


def over_columns(left, right):
    return jnp.dot(left, right, preferred_element_type=F32)


def over_rows(left, right):
    return lax.dot_general(left, right, (((0,), (0,)), ((), ())), preferred_element_type=F32)


def stacked(state, rows):
    return jnp.concatenate(split(state), axis=0), jnp.concatenate([rows, rows], axis=0)


def own_frame(both, early):
    return jnp.where(early, both[:LANES], both[LANES:])


def roll(block, shift):
    return pltpu.roll(block, shift % LANES, axis=1) if shift % LANES else block


def lane_of():
    return lax.broadcasted_iota(jnp.int32, (E, LANES), 1)


def unpack(state_ref, h):
    at, start = divmod(h * E, LANES)
    lane = lane_of()
    parts = []
    for frame in range(2):
        tile = lambda j: state_ref[j * E : (j + 1) * E, frame * LANES : (frame + 1) * LANES]
        block = tile(at)
        if start + E > LANES:
            block = jnp.where(lane >= start, block, tile(at + 1))
        sums = roll(tile(TILES - 1), E - SUMS - 3 * h)
        parts.append(jnp.where(lane < E, roll(block, -start), sums))
    return jnp.concatenate(parts, axis=1)


def packer(state_ref):
    lane = lane_of()
    held = {}

    def put(j, frame, block, start):
        if (j, frame) in held:
            block = jnp.where(lane >= start, block, held[j, frame])
        held[j, frame] = block

    def write(j, frame):
        state_ref[j * E : (j + 1) * E, frame * LANES : (frame + 1) * LANES] = held[j, frame]

    def add(h, block):
        at, start = divmod(h * E, LANES)
        for frame in range(2):
            part = block[:, frame * LANES : (frame + 1) * LANES]
            moved = roll(part, start)
            put(at, frame, moved, start)
            if start + E >= LANES:
                write(at, frame)
            if start + E > LANES:
                put(at + 1, frame, moved, 0)
            put(TILES, frame, roll(part, SUMS + 3 * h - E), SUMS + 3 * h)
            if h == HALF - 1:
                put(TILES - 1, frame, held[TILES, frame], SUMS)
                write(TILES - 1, frame)

    state_ref[TILES * E :, :] = jnp.zeros((STATE_ROWS - TILES * E, WIDE), F32)
    return add


def key_state(key, value, first, second):
    return over_tokens(jnp.maximum(key, 0), by_frame(with_ones(value), first, second))


def key_kernel(ids_ref, key_ref, value_ref, state_ref):
    _, first, second = frame_masks(ids_ref)
    add = packer(state_ref)
    for h in range(HALF):
        rows = pl.ds(h * E, E)
        add(h, key_state(key_ref[rows, :], value_ref[rows, :], first, second))


def query_kernel(half_ref, ids_ref, query_ref, cot_ref, state_ref, aux_ref, grad_state_ref):
    early, first, second = frame_masks(ids_ref)
    for h in range(HALF):
        rows = pl.ds(h * E, E)
        phi = jnp.maximum(query_ref[rows, :], 0)
        numer = own_frame(over_rows(*stacked(unpack(state_ref, h), phi)), early)
        inverse = 1.0 / (numer[E : E + 1] + 1.0)
        wide = cot_ref[rows, :].astype(F32)
        inner = -jnp.sum(wide * numer[:E], axis=0, keepdims=True) * inverse
        aux_ref[h] = jnp.concatenate([inverse, inner], axis=0)
    add = packer(grad_state_ref)
    for h in range(HALF):
        rows = pl.ds(h * E, E)
        inverse, inner = aux_ref[h, 0:1, :], aux_ref[h, 1:2, :]
        phi = by_frame(jnp.maximum(query_ref[rows, :], 0), first, second)
        wide = cot_ref[rows, :].astype(F32)
        high, low = split(with_rows(wide * inverse, inner * inverse))
        block = over_tokens(phi, high) + over_tokens(phi, low)
        add(h, jnp.concatenate([block[:E], block[E:]], axis=1))


def query_grad_kernel(half_ref, ids_ref, query_ref, cot_ref, state_ref, aux_ref, *refs):
    grad_ref = refs[-1]
    _, first, second = frame_masks(ids_ref)
    for h in range(HALF):
        rows = pl.ds(h * E, E)
        high, low = split(unpack(state_ref, h))
        inverse, inner = aux_ref[h, 0:1, :], aux_ref[h, 1:2, :]
        inner_high = inner.astype(BF16).astype(F32)
        inner_mid = (inner - inner_high).astype(BF16).astype(F32)
        inner_low = inner - inner_high - inner_mid
        cots = with_rows(cot_ref[rows, :], inner_high, inner_mid, inner_low)
        cots = by_frame(cots, first, second)
        grad = (over_columns(high, cots) + over_columns(low, cots)) * inverse
        grad_ref[rows, :] = jnp.where(query_ref[rows, :].astype(F32) > 0, grad, 0.0).astype(BF16)


def value_kernel(half_ref, ids_ref, key_ref, value_ref, state_ref, *refs):
    grad_key_ref, grad_value_ref = refs[-2:]
    early, first, second = frame_masks(ids_ref)
    for h in range(HALF):
        rows = pl.ds(h * E, E)
        state = unpack(state_ref, h)
        high, low = split(state)
        key = key_ref[rows, :]
        grad = own_frame(over_rows(*stacked(state, jnp.maximum(key, 0))), early)
        grad_value_ref[rows, :] = grad[:E].astype(BF16)
        values = with_rows(value_ref[rows, :], jnp.ones((1, key.shape[1]), F32))
        values = by_frame(values, first, second)
        grad = over_columns(high, values) + over_columns(low, values)
        grad_key_ref[rows, :] = jnp.where(key.astype(F32) > 0, grad, 0.0).astype(BF16)


def gather_kernel(parts_ref, sum_ref):
    rows, pieces, piece = parts_ref.shape[1], sum_ref.shape[0], sum_ref.shape[1]
    for at in range(pieces):
        filled = min(piece, rows - at * piece)
        if filled > 0:
            here = pl.ds(at * piece, filled)
            total = parts_ref[0, here, :]
            for part in range(1, parts_ref.shape[0]):
                total = total + parts_ref[part, here, :]
            sum_ref[at, :filled, :] = total
        if filled < piece:
            start = max(filled, 0)
            sum_ref[at, start:, :] = jnp.zeros((piece - start, WIDE), F32)


def params():
    return pltpu.CompilerParams(vmem_limit_bytes=VMEM_LIMIT)


def on_half(kernel, half, ids, halves, small, whole, outs):
    tokens = ids.shape[1]
    block = pl.BlockSpec((ROWS, tokens), lambda i, at: (at[0], 0))
    full = lambda shape: pl.BlockSpec(shape, lambda i, at: (0,) * len(shape))
    operands = [ids, *halves, *small, *whole]
    specs = [full(ids.shape)] + [block] * len(halves) + [full(a.shape) for a in small]
    specs += [pl.BlockSpec(memory_space=pl.ANY)] * len(whole)
    aliases = {1 + len(operands) - len(whole) + at: at for at in range(len(whole))}
    shapes = {
        "grad": ((H * E, tokens), BF16),
        "state": ((STATE_ROWS, WIDE), F32),
        "aux": ((HALF, 2, tokens), F32),
    }
    out_shape = [jax.ShapeDtypeStruct(*shapes[out]) for out in outs]
    out_specs = [block if out == "grad" else full(shapes[out][0]) for out in outs]
    return pl.pallas_call(
        kernel,
        out_shape=out_shape,
        grid_spec=pltpu.PrefetchScalarGridSpec(
            num_scalar_prefetch=1, grid=(1,), in_specs=specs, out_specs=out_specs
        ),
        input_output_aliases=aliases,
        compiler_params=params(),
        cost_estimate=pl.CostEstimate(
            flops=2 * 6 * ROWS * WIDE * tokens, bytes_accessed=4 * ROWS * tokens * 2, transcendentals=0
        ),
    )(half, *operands)


def key_states(half, ids, key, value):
    rows = lambda array: lax.dynamic_slice(array, (half[0] * ROWS, 0), (ROWS, array.shape[1]))
    return pl.pallas_call(
        key_kernel,
        out_shape=jax.ShapeDtypeStruct((STATE_ROWS, WIDE), F32),
        compiler_params=params(),
        cost_estimate=pl.CostEstimate(
            flops=2 * ROWS * WIDE * ids.shape[1], bytes_accessed=4 * STATE_ROWS * WIDE, transcendentals=0
        ),
    )(ids, rows(key), rows(value))


def swap_cores(block):
    return lax.ppermute(block, "space", [(i, i ^ 1) for i in range(lax.axis_size("space"))])


def groups(chips_z):
    device = lambda z, y, core: (z * Y + y) * CORES + core
    pairs = range(chips_z // 2)
    near = [
        [device(2 * pair + i, y, core) for i in range(2) for y in range(Y)]
        for core in range(CORES) for pair in pairs
    ]
    far = [
        [device(2 * pair + i, y, core) for pair in pairs]
        for core in range(CORES) for i in range(2) for y in range(Y)
    ]
    return near, far


def exchange(block, members):
    return lax.all_to_all(block, "space", 0, 0, axis_index_groups=members, tiled=False)


def carried(summed, backward):
    frames = lax.axis_size("frames")
    near, far = groups(lax.axis_size("space") // (Y * CORES))
    chips, places = len(near[0]), len(far[0])
    rows = summed.shape[0] // chips
    part = -(-rows // (8 * places)) * 8
    summed = exchange(summed.reshape(chips, rows, WIDE), near)
    summed = pl.pallas_call(
        gather_kernel,
        out_shape=jax.ShapeDtypeStruct((places, part, WIDE), F32),
        compiler_params=params(),
    )(summed)
    summed = jnp.sum(exchange(summed, far), axis=0)
    frame0, frame1 = summed[:, :LANES], summed[:, LANES:]
    total = frame0 + frame1
    me = lax.axis_index("frames")
    carry = jnp.zeros_like(total)
    arrived = []
    for hop in range(1, frames):
        step = -hop if backward else hop
        arrived.append(
            lax.ppermute(total, "frames", [(i, (i + step) % frames) for i in range(frames)])
        )
    for hop, moved in enumerate(arrived, 1):
        reaches = (me + hop < frames) if backward else (me >= hop)
        carry = carry + jnp.where(reaches, moved, 0.0)
    if backward:
        done = jnp.concatenate([carry + total, carry + frame1], axis=1)
    else:
        done = jnp.concatenate([carry + frame0, carry + total], axis=1)
    done = exchange(jnp.broadcast_to(done[None], (places,) + done.shape), far)
    done = done.reshape(places * part, WIDE)[:rows]
    done = exchange(jnp.broadcast_to(done[None], (chips,) + done.shape), near)
    return done.reshape(chips * rows, WIDE)


def on_device(queries, key_inputs, value_inputs, out_cotangent, frame_ids):
    ids = frame_ids.reshape(1, -1)
    query, key, value, cot = (a.T for a in (queries, key_inputs, value_inputs, out_cotangent))
    core = (lax.axis_index("space") % CORES).astype(jnp.int32).reshape(1)
    there = 1 - core
    send = key_states(there, ids, key, value)
    received = swap_cores(send)
    keep = key_states(core, ids, key, value)
    mine = carried(keep + received, False)
    other = swap_cores(mine)
    aux_mine, keep = on_half(query_kernel, core, ids, (query, cot), (mine,), (), ("aux", "state"))
    other, keep = lax.optimization_barrier((other, keep))
    aux, send = on_half(query_kernel, there, ids, (query, cot), (other,), (), ("aux", "state"))
    received = swap_cores(send)
    late, late_other, _ = lax.optimization_barrier((mine, other, send))
    grads = on_half(query_grad_kernel, core, ids, (query, cot), (late, aux_mine), (), ("grad",))
    (grad_query,) = on_half(
        query_grad_kernel, there, ids, (query, cot), (late_other, aux), grads, ("grad",)
    )
    received, grad_query = lax.optimization_barrier((received, grad_query))
    last = carried(keep + received, True)
    last_other = swap_cores(last)
    grads = on_half(value_kernel, core, ids, (key, value), (last,), (), ("grad", "grad"))
    grad_key, grad_value = on_half(
        value_kernel, there, ids, (key, value), (last_other,), grads, ("grad", "grad")
    )
    return grad_query.T, grad_key.T, grad_value.T


def solution(mesh):
    rows = P(("frames", "space"), None)
    return jax.shard_map(
        on_device,
        mesh=mesh,
        in_specs=(rows, rows, rows, rows, P(("frames", "space"))),
        out_specs=(rows, rows, rows),
        check_vma=False,
    )
```

```python
import jax
import jax.numpy as jnp
from jax import lax
from jax.experimental import pallas as pl
from jax.experimental.pallas import tpu as pltpu
from jax.sharding import PartitionSpec as P

H = 20
E = 112
LANES = 128
CORES = 2
HALF = H // CORES
ROWS = HALF * E
TILES = -(-ROWS // 128)
SUMS = ROWS % 128
GROUP = 5
STATE_ROWS = 1024
WIDE = 2 * LANES
F32 = jnp.float32
BF16 = jnp.bfloat16
VMEM_LIMIT = 32 * 1024 * 1024
Y = 4


def frame_masks(ids_ref):
    early = ids_ref[...] == 0
    first = early.astype(F32)
    return early, first.astype(BF16), (1.0 - first).astype(BF16)


def by_frame(rows, first, second):
    return jnp.concatenate([rows * first, rows * second], axis=0)


def split(values):
    high = values.astype(BF16)
    return high, (values - high.astype(F32)).astype(BF16)


def with_ones(rows):
    return jnp.concatenate([rows, jnp.ones((LANES - E, rows.shape[1]), rows.dtype)], axis=0)


def sums_of(h):
    return 3 * (h % GROUP)


def with_rows(rows, h, *extra):
    at = lax.broadcasted_iota(jnp.int32, (LANES - E, rows.shape[1]), 0)
    tail = jnp.zeros((LANES - E, rows.shape[1]), F32)
    for place, row in enumerate(extra, sums_of(h)):
        tail = jnp.where(at == place, row, tail)
    return jnp.concatenate([rows, tail.astype(rows.dtype)], axis=0)


def over_tokens(left, right):
    return lax.dot_general(left, right, (((1,), (1,)), ((), ())), preferred_element_type=F32)


def over_columns(left, right):
    return jnp.dot(left, right, preferred_element_type=F32)


def over_rows(left, right):
    return lax.dot_general(left, right, (((0,), (0,)), ((), ())), preferred_element_type=F32)


def stacked(state, rows):
    return jnp.concatenate(split(state), axis=0), jnp.concatenate([rows, rows], axis=0)


def own_frame(both, early):
    return jnp.where(early, both[:LANES], both[LANES:])


def roll(block, shift):
    return pltpu.roll(block, shift % LANES, axis=1) if shift % LANES else block


def lane_of():
    return lax.broadcasted_iota(jnp.int32, (E, LANES), 1)


def unpacker(state_ref):
    lane = lane_of()

    def tile(j, frame):
        return state_ref[j * E : (j + 1) * E, frame * LANES : (frame + 1) * LANES]

    last = [tile(TILES - 1, frame) for frame in range(2)]
    sums = (last, [roll(block, LANES - E) for block in last])

    def get(h):
        at, start = divmod(h * E, LANES)
        parts = []
        for frame in range(2):
            block = tile(at, frame)
            if start + E > LANES:
                block = jnp.where(lane >= start, block, tile(at + 1, frame))
            parts.append(jnp.where(lane < E, roll(block, -start), sums[h // GROUP][frame]))
        return jnp.concatenate(parts, axis=1)

    return get


def packer(state_ref):
    lane = lane_of()
    held = {}

    def put(j, frame, block, start):
        if (j, frame) in held:
            block = jnp.where(lane >= start, block, held[j, frame])
        held[j, frame] = block

    def write(j, frame):
        state_ref[j * E : (j + 1) * E, frame * LANES : (frame + 1) * LANES] = held[j, frame]

    def add(h, block):
        at, start = divmod(h * E, LANES)
        for frame in range(2):
            part = block[:, frame * LANES : (frame + 1) * LANES]
            moved = roll(part, start)
            put(at, frame, moved, start)
            if start + E >= LANES:
                write(at, frame)
            if start + E > LANES:
                put(at + 1, frame, moved, 0)
            put(TILES + h // GROUP, frame, part, E + sums_of(h))
            if h == HALF - 1:
                put(TILES - 1, frame, roll(held[TILES + 1, frame], E - LANES), SUMS)
                put(TILES - 1, frame, held[TILES, frame], E)
                write(TILES - 1, frame)

    state_ref[TILES * E :, :] = jnp.zeros((STATE_ROWS - TILES * E, WIDE), F32)
    return add


def key_state(key, value, first, second):
    return over_tokens(jnp.maximum(key, 0), by_frame(with_ones(value), first, second))


def key_kernel(ids_ref, key_ref, value_ref, state_ref):
    _, first, second = frame_masks(ids_ref)
    add = packer(state_ref)
    for h in range(HALF):
        rows = pl.ds(h * E, E)
        add(h, key_state(key_ref[rows, :], value_ref[rows, :], first, second))


def query_kernel(half_ref, ids_ref, query_ref, cot_ref, state_ref, aux_ref, grad_state_ref):
    early, first, second = frame_masks(ids_ref)
    state_of = unpacker(state_ref)
    for h in range(HALF):
        rows = pl.ds(h * E, E)
        phi = jnp.maximum(query_ref[rows, :], 0)
        numer = own_frame(over_rows(*stacked(state_of(h), phi)), early)
        inverse = 1.0 / (numer[E + sums_of(h) : E + sums_of(h) + 1] + 1.0)
        wide = cot_ref[rows, :].astype(F32)
        inner = -jnp.sum(wide * numer[:E], axis=0, keepdims=True) * inverse
        aux_ref[h] = jnp.concatenate([inverse, inner], axis=0)
    add = packer(grad_state_ref)
    for h in range(HALF):
        rows = pl.ds(h * E, E)
        inverse, inner = aux_ref[h, 0:1, :], aux_ref[h, 1:2, :]
        phi = by_frame(jnp.maximum(query_ref[rows, :], 0), first, second)
        wide = cot_ref[rows, :].astype(F32)
        high, low = split(with_rows(wide * inverse, h, inner * inverse))
        block = over_tokens(phi, high) + over_tokens(phi, low)
        add(h, jnp.concatenate([block[:E], block[E:]], axis=1))


def query_grad_kernel(half_ref, ids_ref, query_ref, cot_ref, state_ref, aux_ref, *refs):
    grad_ref = refs[-1]
    _, first, second = frame_masks(ids_ref)
    state_of = unpacker(state_ref)
    for h in range(HALF):
        rows = pl.ds(h * E, E)
        high, low = split(state_of(h))
        inverse, inner = aux_ref[h, 0:1, :], aux_ref[h, 1:2, :]
        inner_high = inner.astype(BF16).astype(F32)
        inner_mid = (inner - inner_high).astype(BF16).astype(F32)
        inner_low = inner - inner_high - inner_mid
        cots = with_rows(cot_ref[rows, :], h, inner_high, inner_mid, inner_low)
        cots = by_frame(cots, first, second)
        grad = (over_columns(high, cots) + over_columns(low, cots)) * inverse
        grad_ref[rows, :] = jnp.where(query_ref[rows, :].astype(F32) > 0, grad, 0.0).astype(BF16)


def value_kernel(half_ref, ids_ref, key_ref, value_ref, state_ref, *refs):
    grad_key_ref, grad_value_ref = refs[-2:]
    early, first, second = frame_masks(ids_ref)
    state_of = unpacker(state_ref)
    for h in range(HALF):
        rows = pl.ds(h * E, E)
        state = state_of(h)
        high, low = split(state)
        key = key_ref[rows, :]
        grad = own_frame(over_rows(*stacked(state, jnp.maximum(key, 0))), early)
        grad_value_ref[rows, :] = grad[:E].astype(BF16)
        values = with_rows(value_ref[rows, :], h, jnp.ones((1, key.shape[1]), F32))
        values = by_frame(values, first, second)
        grad = over_columns(high, values) + over_columns(low, values)
        grad_key_ref[rows, :] = jnp.where(key.astype(F32) > 0, grad, 0.0).astype(BF16)


def gather_kernel(parts_ref, sum_ref):
    rows, pieces, piece = parts_ref.shape[1], sum_ref.shape[0], sum_ref.shape[1]
    for at in range(pieces):
        filled = min(piece, rows - at * piece)
        if filled > 0:
            here = pl.ds(at * piece, filled)
            total = parts_ref[0, here, :]
            for part in range(1, parts_ref.shape[0]):
                total = total + parts_ref[part, here, :]
            sum_ref[at, :filled, :] = total
        if filled < piece:
            start = max(filled, 0)
            sum_ref[at, start:, :] = jnp.zeros((piece - start, WIDE), F32)


def params():
    return pltpu.CompilerParams(vmem_limit_bytes=VMEM_LIMIT)


def on_half(kernel, half, ids, halves, small, whole, outs):
    tokens = ids.shape[1]
    block = pl.BlockSpec((ROWS, tokens), lambda i, at: (at[0], 0))
    full = lambda shape: pl.BlockSpec(shape, lambda i, at: (0,) * len(shape))
    operands = [ids, *halves, *small, *whole]
    specs = [full(ids.shape)] + [block] * len(halves) + [full(a.shape) for a in small]
    specs += [pl.BlockSpec(memory_space=pl.ANY)] * len(whole)
    aliases = {1 + len(operands) - len(whole) + at: at for at in range(len(whole))}
    shapes = {
        "grad": ((H * E, tokens), BF16),
        "state": ((STATE_ROWS, WIDE), F32),
        "aux": ((HALF, 2, tokens), F32),
    }
    out_shape = [jax.ShapeDtypeStruct(*shapes[out]) for out in outs]
    out_specs = [block if out == "grad" else full(shapes[out][0]) for out in outs]
    return pl.pallas_call(
        kernel,
        out_shape=out_shape,
        grid_spec=pltpu.PrefetchScalarGridSpec(
            num_scalar_prefetch=1, grid=(1,), in_specs=specs, out_specs=out_specs
        ),
        input_output_aliases=aliases,
        compiler_params=params(),
        cost_estimate=pl.CostEstimate(
            flops=2 * 6 * ROWS * WIDE * tokens, bytes_accessed=4 * ROWS * tokens * 2, transcendentals=0
        ),
    )(half, *operands)


def key_states(half, ids, key, value):
    rows = lambda array: lax.dynamic_slice(array, (half[0] * ROWS, 0), (ROWS, array.shape[1]))
    return pl.pallas_call(
        key_kernel,
        out_shape=jax.ShapeDtypeStruct((STATE_ROWS, WIDE), F32),
        compiler_params=params(),
        cost_estimate=pl.CostEstimate(
            flops=2 * ROWS * WIDE * ids.shape[1], bytes_accessed=4 * STATE_ROWS * WIDE, transcendentals=0
        ),
    )(ids, rows(key), rows(value))


def swap_cores(block):
    return lax.ppermute(block, "space", [(i, i ^ 1) for i in range(lax.axis_size("space"))])


def groups(chips_z):
    device = lambda z, y, core: (z * Y + y) * CORES + core
    pairs = range(chips_z // 2)
    near = [
        [device(2 * pair + i, y, core) for i in range(2) for y in range(Y)]
        for core in range(CORES) for pair in pairs
    ]
    far = [
        [device(2 * pair + i, y, core) for pair in pairs]
        for core in range(CORES) for i in range(2) for y in range(Y)
    ]
    return near, far


def exchange(block, members):
    return lax.all_to_all(block, "space", 0, 0, axis_index_groups=members, tiled=False)


def carried(summed, backward):
    frames = lax.axis_size("frames")
    near, far = groups(lax.axis_size("space") // (Y * CORES))
    chips, places = len(near[0]), len(far[0])
    rows = summed.shape[0] // chips
    part = -(-rows // (8 * places)) * 8
    summed = exchange(summed.reshape(chips, rows, WIDE), near)
    summed = pl.pallas_call(
        gather_kernel,
        out_shape=jax.ShapeDtypeStruct((places, part, WIDE), F32),
        compiler_params=params(),
    )(summed)
    summed = jnp.sum(exchange(summed, far), axis=0)
    frame0, frame1 = summed[:, :LANES], summed[:, LANES:]
    total = frame0 + frame1
    me = lax.axis_index("frames")
    carry = jnp.zeros_like(total)
    arrived = []
    for hop in range(1, frames):
        step = -hop if backward else hop
        arrived.append(
            lax.ppermute(total, "frames", [(i, (i + step) % frames) for i in range(frames)])
        )
    for hop, moved in enumerate(arrived, 1):
        reaches = (me + hop < frames) if backward else (me >= hop)
        carry = carry + jnp.where(reaches, moved, 0.0)
    if backward:
        done = jnp.concatenate([carry + total, carry + frame1], axis=1)
    else:
        done = jnp.concatenate([carry + frame0, carry + total], axis=1)
    done = exchange(jnp.broadcast_to(done[None], (places,) + done.shape), far)
    done = done.reshape(places * part, WIDE)[:rows]
    done = exchange(jnp.broadcast_to(done[None], (chips,) + done.shape), near)
    return done.reshape(chips * rows, WIDE)


def on_device(queries, key_inputs, value_inputs, out_cotangent, frame_ids):
    ids = frame_ids.reshape(1, -1)
    query, key, value, cot = (a.T for a in (queries, key_inputs, value_inputs, out_cotangent))
    core = (lax.axis_index("space") % CORES).astype(jnp.int32).reshape(1)
    there = 1 - core
    send = key_states(there, ids, key, value)
    received = swap_cores(send)
    keep = key_states(core, ids, key, value)
    mine = carried(keep + received, False)
    other = swap_cores(mine)
    aux_mine, keep = on_half(query_kernel, core, ids, (query, cot), (mine,), (), ("aux", "state"))
    other, keep = lax.optimization_barrier((other, keep))
    aux, send = on_half(query_kernel, there, ids, (query, cot), (other,), (), ("aux", "state"))
    received = swap_cores(send)
    late, late_other, _ = lax.optimization_barrier((mine, other, send))
    grads = on_half(query_grad_kernel, core, ids, (query, cot), (late, aux_mine), (), ("grad",))
    (grad_query,) = on_half(
        query_grad_kernel, there, ids, (query, cot), (late_other, aux), grads, ("grad",)
    )
    received, grad_query = lax.optimization_barrier((received, grad_query))
    last = carried(keep + received, True)
    last_other = swap_cores(last)
    grads = on_half(value_kernel, core, ids, (key, value), (last,), (), ("grad", "grad"))
    grad_key, grad_value = on_half(
        value_kernel, there, ids, (key, value), (last_other,), grads, ("grad", "grad")
    )
    return grad_query.T, grad_key.T, grad_value.T


def solution(mesh):
    rows = P(("frames", "space"), None)
    return jax.shard_map(
        on_device,
        mesh=mesh,
        in_specs=(rows, rows, rows, rows, P(("frames", "space"))),
        out_specs=(rows, rows, rows),
        check_vma=False,
    )
```

```python
import jax
import jax.numpy as jnp
from jax import lax
from jax.experimental import pallas as pl
from jax.experimental.pallas import tpu as pltpu
from jax.sharding import PartitionSpec as P

H = 20
E = 112
LANES = 128
CORES = 2
HALF = H // CORES
ROWS = HALF * E
TILES = -(-ROWS // 128)
SUMS = ROWS % 128
GROUP = 5
STATE_ROWS = 1024
WIDE = 2 * LANES
F32 = jnp.float32
BF16 = jnp.bfloat16
VMEM_LIMIT = 32 * 1024 * 1024
Y = 4


def frame_masks(ids_ref):
    early = ids_ref[...] == 0
    first = early.astype(F32)
    return early, first.astype(BF16), (1.0 - first).astype(BF16)


def by_frame(rows, first, second):
    return jnp.concatenate([rows * first, rows * second], axis=0)


def split(values):
    high = values.astype(BF16)
    return high, (values - high.astype(F32)).astype(BF16)


def with_ones(rows):
    return jnp.concatenate([rows, jnp.ones((LANES - E, rows.shape[1]), rows.dtype)], axis=0)


def sums_of(h):
    return 3 * (h % GROUP)


def with_rows(rows, h, *extra):
    at = lax.broadcasted_iota(jnp.int32, (LANES - E, rows.shape[1]), 0)
    tail = jnp.zeros((LANES - E, rows.shape[1]), F32)
    for place, row in enumerate(extra, sums_of(h)):
        tail = jnp.where(at == place, row, tail)
    return jnp.concatenate([rows, tail.astype(rows.dtype)], axis=0)


def over_tokens(left, right):
    return lax.dot_general(left, right, (((1,), (1,)), ((), ())), preferred_element_type=F32)


def over_columns(left, right):
    return jnp.dot(left, right, preferred_element_type=F32)


def over_rows(left, right):
    return lax.dot_general(left, right, (((0,), (0,)), ((), ())), preferred_element_type=F32)


def stacked(state, rows):
    return jnp.concatenate(split(state), axis=0), jnp.concatenate([rows, rows], axis=0)


def own_frame(both, early):
    return jnp.where(early, both[:LANES], both[LANES:])


def roll(block, shift):
    return pltpu.roll(block, shift % LANES, axis=1) if shift % LANES else block


def lane_of():
    return lax.broadcasted_iota(jnp.int32, (E, LANES), 1)


def unpacker(state_ref):
    lane = lane_of()

    def tile(j, frame):
        return state_ref[j * E : (j + 1) * E, frame * LANES : (frame + 1) * LANES]

    last = [tile(TILES - 1, frame) for frame in range(2)]
    sums = (last, [roll(block, LANES - E) for block in last])

    def get(h):
        at, start = divmod(h * E, LANES)
        parts = []
        for frame in range(2):
            block = tile(at, frame)
            if start + E > LANES:
                block = jnp.where(lane >= start, block, tile(at + 1, frame))
            parts.append(jnp.where(lane < E, roll(block, -start), sums[h // GROUP][frame]))
        return jnp.concatenate(parts, axis=1)

    return get


def packer(state_ref):
    lane = lane_of()
    held = {}

    def put(j, frame, block, start):
        if (j, frame) in held:
            block = jnp.where(lane >= start, block, held[j, frame])
        held[j, frame] = block

    def write(j, frame):
        state_ref[j * E : (j + 1) * E, frame * LANES : (frame + 1) * LANES] = held[j, frame]

    def add(h, block):
        at, start = divmod(h * E, LANES)
        for frame in range(2):
            part = block[:, frame * LANES : (frame + 1) * LANES]
            moved = roll(part, start)
            put(at, frame, moved, start)
            if start + E >= LANES:
                write(at, frame)
            if start + E > LANES:
                put(at + 1, frame, moved, 0)
            put(TILES + h // GROUP, frame, part, E + sums_of(h))
            if h == HALF - 1:
                put(TILES - 1, frame, roll(held[TILES + 1, frame], E - LANES), SUMS)
                put(TILES - 1, frame, held[TILES, frame], E)
                write(TILES - 1, frame)

    state_ref[TILES * E :, :] = jnp.zeros((STATE_ROWS - TILES * E, WIDE), F32)
    return add


def key_state(key, value, first, second):
    return over_tokens(jnp.maximum(key, 0), by_frame(with_ones(value), first, second))


def key_kernel(ids_ref, key_ref, value_ref, state_ref):
    _, first, second = frame_masks(ids_ref)
    add = packer(state_ref)
    for h in range(HALF):
        rows = pl.ds(h * E, E)
        add(h, key_state(key_ref[rows, :], value_ref[rows, :], first, second))


def query_kernel(half_ref, ids_ref, query_ref, cot_ref, state_ref, aux_ref, grad_state_ref):
    early, first, second = frame_masks(ids_ref)
    state_of = unpacker(state_ref)
    for h in range(HALF):
        rows = pl.ds(h * E, E)
        phi = jnp.maximum(query_ref[rows, :], 0)
        numer = own_frame(over_rows(*stacked(state_of(h), phi)), early)
        inverse = 1.0 / (numer[E + sums_of(h) : E + sums_of(h) + 1] + 1.0)
        wide = cot_ref[rows, :].astype(F32)
        inner = -jnp.sum(wide * numer[:E], axis=0, keepdims=True) * inverse
        aux_ref[h] = jnp.concatenate([inverse, inner], axis=0)
    add = packer(grad_state_ref)
    for h in range(HALF):
        rows = pl.ds(h * E, E)
        inverse, inner = aux_ref[h, 0:1, :], aux_ref[h, 1:2, :]
        phi = by_frame(jnp.maximum(query_ref[rows, :], 0), first, second)
        wide = cot_ref[rows, :].astype(F32)
        high, low = split(with_rows(wide * inverse, h, inner * inverse))
        block = over_tokens(phi, high) + over_tokens(phi, low)
        add(h, jnp.concatenate([block[:E], block[E:]], axis=1))


def query_grad_kernel(half_ref, ids_ref, query_ref, cot_ref, state_ref, aux_ref, *refs):
    grad_ref = refs[-1]
    _, first, second = frame_masks(ids_ref)
    state_of = unpacker(state_ref)
    for h in range(HALF):
        rows = pl.ds(h * E, E)
        high, low = split(state_of(h))
        inverse, inner = aux_ref[h, 0:1, :], aux_ref[h, 1:2, :]
        inner_high = inner.astype(BF16).astype(F32)
        inner_mid = (inner - inner_high).astype(BF16).astype(F32)
        inner_low = inner - inner_high - inner_mid
        cots = with_rows(cot_ref[rows, :], h, inner_high, inner_mid, inner_low)
        cots = by_frame(cots, first, second)
        grad = (over_columns(high, cots) + over_columns(low, cots)) * inverse
        grad_ref[rows, :] = jnp.where(query_ref[rows, :].astype(F32) > 0, grad, 0.0).astype(BF16)


def value_kernel(half_ref, ids_ref, key_ref, value_ref, state_ref, *refs):
    grad_key_ref, grad_value_ref = refs[-2:]
    early, first, second = frame_masks(ids_ref)
    state_of = unpacker(state_ref)
    for h in range(HALF):
        rows = pl.ds(h * E, E)
        state = state_of(h)
        high, low = split(state)
        key = key_ref[rows, :]
        grad = own_frame(over_rows(*stacked(state, jnp.maximum(key, 0))), early)
        grad_value_ref[rows, :] = grad[:E].astype(BF16)
        values = with_rows(value_ref[rows, :], h, jnp.ones((1, key.shape[1]), F32))
        values = by_frame(values, first, second)
        grad = over_columns(high, values) + over_columns(low, values)
        grad_key_ref[rows, :] = jnp.where(key.astype(F32) > 0, grad, 0.0).astype(BF16)


def gather_kernel(parts_ref, sum_ref):
    rows, pieces, piece = parts_ref.shape[1], sum_ref.shape[0], sum_ref.shape[1]
    for at in range(pieces):
        filled = min(piece, rows - at * piece)
        if filled > 0:
            here = pl.ds(at * piece, filled)
            total = parts_ref[0, here, :]
            for part in range(1, parts_ref.shape[0]):
                total = total + parts_ref[part, here, :]
            sum_ref[at, :filled, :] = total
        if filled < piece:
            start = max(filled, 0)
            sum_ref[at, start:, :] = jnp.zeros((piece - start, WIDE), F32)


def params():
    return pltpu.CompilerParams(vmem_limit_bytes=VMEM_LIMIT)


def on_half(kernel, half, ids, halves, small, whole, outs):
    tokens = ids.shape[1]
    block = pl.BlockSpec((ROWS, tokens), lambda i, at: (at[0], 0))
    full = lambda shape: pl.BlockSpec(shape, lambda i, at: (0,) * len(shape))
    operands = [ids, *halves, *small, *whole]
    specs = [full(ids.shape)] + [block] * len(halves) + [full(a.shape) for a in small]
    specs += [pl.BlockSpec(memory_space=pl.ANY)] * len(whole)
    aliases = {1 + len(operands) - len(whole) + at: at for at in range(len(whole))}
    shapes = {
        "grad": ((H * E, tokens), BF16),
        "state": ((STATE_ROWS, WIDE), F32),
        "aux": ((HALF, 2, tokens), F32),
    }
    out_shape = [jax.ShapeDtypeStruct(*shapes[out]) for out in outs]
    out_specs = [block if out == "grad" else full(shapes[out][0]) for out in outs]
    return pl.pallas_call(
        kernel,
        out_shape=out_shape,
        grid_spec=pltpu.PrefetchScalarGridSpec(
            num_scalar_prefetch=1, grid=(1,), in_specs=specs, out_specs=out_specs
        ),
        input_output_aliases=aliases,
        compiler_params=params(),
        cost_estimate=pl.CostEstimate(
            flops=2 * 6 * ROWS * WIDE * tokens, bytes_accessed=4 * ROWS * tokens * 2, transcendentals=0
        ),
    )(half, *operands)


def key_states(half, ids, key, value):
    rows = lambda array: lax.dynamic_slice(array, (half[0] * ROWS, 0), (ROWS, array.shape[1]))
    return pl.pallas_call(
        key_kernel,
        out_shape=jax.ShapeDtypeStruct((STATE_ROWS, WIDE), F32),
        compiler_params=params(),
        cost_estimate=pl.CostEstimate(
            flops=2 * ROWS * WIDE * ids.shape[1], bytes_accessed=4 * STATE_ROWS * WIDE, transcendentals=0
        ),
    )(ids, rows(key), rows(value))


def swap_cores(block):
    return lax.ppermute(block, "space", [(i, i ^ 1) for i in range(lax.axis_size("space"))])


def groups(chips_z):
    device = lambda z, y, core: (z * Y + y) * CORES + core
    pairs = range(chips_z // 2)
    near = [
        [device(2 * pair + i, y, core) for i in range(2) for y in range(Y)]
        for core in range(CORES) for pair in pairs
    ]
    far = [
        [device(2 * pair + i, y, core) for pair in pairs]
        for core in range(CORES) for i in range(2) for y in range(Y)
    ]
    return near, far


def exchange(block, members):
    return lax.all_to_all(block, "space", 0, 0, axis_index_groups=members, tiled=False)


def carried(summed, backward):
    frames = lax.axis_size("frames")
    near, far = groups(lax.axis_size("space") // (Y * CORES))
    chips, places = len(near[0]), len(far[0])
    rows = summed.shape[0] // chips
    part = -(-rows // (8 * places)) * 8
    summed = exchange(summed.reshape(chips, rows, WIDE), near)
    summed = pl.pallas_call(
        gather_kernel,
        out_shape=jax.ShapeDtypeStruct((places, part, WIDE), F32),
        compiler_params=params(),
    )(summed)
    summed = jnp.sum(exchange(summed, far), axis=0)
    frame0, frame1 = summed[:, :LANES], summed[:, LANES:]
    total = frame0 + frame1
    me = lax.axis_index("frames")
    carry = jnp.zeros_like(total)
    arrived = []
    for hop in range(1, frames):
        step = -hop if backward else hop
        arrived.append(
            lax.ppermute(total, "frames", [(i, (i + step) % frames) for i in range(frames)])
        )
    for hop, moved in enumerate(arrived, 1):
        reaches = (me + hop < frames) if backward else (me >= hop)
        carry = carry + jnp.where(reaches, moved, 0.0)
    if backward:
        done = jnp.concatenate([carry + total, carry + frame1], axis=1)
    else:
        done = jnp.concatenate([carry + frame0, carry + total], axis=1)
    done = exchange(jnp.broadcast_to(done[None], (places,) + done.shape), far)
    done = done.reshape(places * part, WIDE)[:rows]
    done = exchange(jnp.broadcast_to(done[None], (chips,) + done.shape), near)
    return done.reshape(chips * rows, WIDE)


def on_device(queries, key_inputs, value_inputs, out_cotangent, frame_ids):
    ids = frame_ids.reshape(1, -1)
    query, key, value, cot = (a.T for a in (queries, key_inputs, value_inputs, out_cotangent))
    core = (lax.axis_index("space") % CORES).astype(jnp.int32).reshape(1)
    there = 1 - core
    send = key_states(there, ids, key, value)
    received = swap_cores(send)
    own, _ = lax.optimization_barrier((core, send))
    keep = key_states(own, ids, key, value)
    mine = carried(keep + received, False)
    other = swap_cores(mine)
    aux_mine, keep = on_half(query_kernel, core, ids, (query, cot), (mine,), (), ("aux", "state"))
    other, keep = lax.optimization_barrier((other, keep))
    aux, send = on_half(query_kernel, there, ids, (query, cot), (other,), (), ("aux", "state"))
    received = swap_cores(send)
    late, late_other, _ = lax.optimization_barrier((mine, other, send))
    grads = on_half(query_grad_kernel, core, ids, (query, cot), (late, aux_mine), (), ("grad",))
    (grad_query,) = on_half(
        query_grad_kernel, there, ids, (query, cot), (late_other, aux), grads, ("grad",)
    )
    received, grad_query = lax.optimization_barrier((received, grad_query))
    last = carried(keep + received, True)
    last_other = swap_cores(last)
    grads = on_half(value_kernel, core, ids, (key, value), (last,), (), ("grad", "grad"))
    grad_key, grad_value = on_half(
        value_kernel, there, ids, (key, value), (last_other,), grads, ("grad", "grad")
    )
    return grad_query.T, grad_key.T, grad_value.T


def solution(mesh):
    rows = P(("frames", "space"), None)
    return jax.shard_map(
        on_device,
        mesh=mesh,
        in_specs=(rows, rows, rows, rows, P(("frames", "space"))),
        out_specs=(rows, rows, rows),
        check_vma=False,
    )
```
